32 devices in a mesh: panel: 8 (over z, x), obs: 4 (over y, core).
Axes of the slice: x: 2, y: 2, z: 4, core: 2. Of those that a mesh axis runs over, the one named last changes fastest.
Arguments:
- samples: bfloat16 [1024, 4, 4096], P(('panel', 'obs')), may hold values from -6 to 6
- panel_position: float32 [3, 4096], P(None, 'panel'), may hold values from -1 to 1
- panel_area: float32 [4096], P('panel'), may hold values from 0.5 to 2
- panel_counts: int32 [32], P('panel'), may hold values from 1 to 128
- obs_position: float32 [3, 1024], P(None, 'obs'), may hold values from -12 to 12, as said below
- freq_bins: int32 [32], replicated, may hold values from 1 to 511
Outputs:
- far_pressure: float32 [2, 32, 1024], P(None, None, ('obs', 'panel'))
The draws below stay inside these ranges and needn't reach their ends.
Inputs may be any that keep to these rules, and one draw needn't show every extreme that they name: `obs_position`: observers lie at distances 6 to 12 from the anchor.
All inputs are finite; a program needn't handle non-finite values.
Results may differ from the reference program's by a relative error of at most 0.0027.
Values may be sent and summed in bfloat16 or wider, within the bound.
A program may use at most 64 MiB of HBM per device.

```python
import math
import jax
import jax.numpy as jnp
from jax import lax

TIME = 1024
NF = 32
FBLK = 4
PANELS = 4096
OBS = 1024
NBLK = 32


def draw_obs_position(key, part):
    subkeys = jax.random.split(jax.random.fold_in(key, 11), 3)
    height = jax.random.uniform(subkeys[0], (OBS,), jnp.float32, -1.0, 1.0)
    azimuth = jax.random.uniform(subkeys[1], (OBS,), jnp.float32, -math.pi, math.pi)
    radius = jax.random.uniform(subkeys[2], (OBS,), jnp.float32, 6.0, 12.0)
    cycle_radius = radius * jnp.sqrt(jnp.maximum(1.0 - height * height, 0.0))
    return jnp.stack([cycle_radius * jnp.cos(azimuth), cycle_radius * jnp.sin(azimuth), radius * height])


def touch_ends(array, stream_key, smallest, top_value):
    longest = array.shape.index(max(array.shape))
    spots = []
    for shift in (0, 1):
        where = [jax.random.randint(jax.random.fold_in(stream_key, axis), (), 0, length) for axis, length in enumerate(array.shape)]
        where[longest] = (where[longest] + shift) % array.shape[longest]
        spots.append(tuple(where))
    return array.at[spots[0]].set(smallest).at[spots[1]].set(top_value)


def steps_of(own_key, shape, shards, smallest, top_value):
    loudness = 1.0
    for position, shards_of in shards:
        draws = jax.random.uniform(jax.random.fold_in(jax.random.fold_in(own_key, 6), position), (shards_of,), jnp.float32, smallest / len(shards), top_value / len(shards))
        loudness = loudness * jnp.repeat(jnp.exp(draws), shape[position] // shards_of).reshape((-1,) + (1,) * (len(shape) - 1 - position))
    return loudness


def centred(key, shape, deviation, most, cuts=(), kind=jnp.bfloat16):
    level = steps_of(key, shape, cuts, -0.22, 0.18) if cuts else 1.0
    values = jax.random.normal(key, shape, jnp.float32) * deviation * level
    return jnp.minimum(jnp.maximum(values, -most), most).astype(kind)


def setup_inputs(seed: int = 0) -> dict:
    splits = jax.random.split(jax.random.key(seed), 7)
    return {
        "samples": centred(splits[0], (TIME, 4, PANELS), 1.0, 6.0, ((0, 32),)),
        "panel_position": jnp.clip(jax.random.uniform(splits[1], (3, PANELS), jnp.float32, -1.0, 1.0) * steps_of(splits[1], (3, PANELS), ((1, 8),), -0.4, 0.0), -1.0, 1.0),
        "panel_area": jnp.clip(jnp.exp(math.log(2.0) - 1.3862944 * jax.random.uniform(splits[2], (PANELS,), jnp.float32) ** steps_of(splits[2], (PANELS,), ((0, 8),), -0.2, 0.2)), 0.5, 2.0),
        "panel_counts": touch_ends(jax.random.randint(splits[3], (NBLK,), 1, 129), jax.random.fold_in(splits[3], 1), 1, 128).astype(jnp.int32),
        "obs_position": draw_obs_position(jax.random.fold_in(splits[6], 71), 0),
        "freq_bins": touch_ends(jax.random.randint(splits[5], (NF,), 1, TIME // 2), jax.random.fold_in(splits[5], 1), 1, (TIME // 2) - 1).astype(jnp.int32),
    }


SPACING = 0.1

def make_table(time_rows, freq_bins):
    phase_index = freq_bins[None, :] * time_rows[:, None] % TIME
    angle_arg = 2.0 * math.pi / TIME * phase_index.astype(jnp.float32)
    window = 0.5 - 0.5 * jnp.cos(2.0 * math.pi / TIME * time_rows.astype(jnp.float32))
    weight = 2.0 / TIME * window[:, None]
    return jnp.concatenate([weight * jnp.cos(angle_arg), -weight * jnp.sin(angle_arg)], axis=1).astype(jnp.bfloat16)

def live_rows(counts):
    lane_ids = jnp.arange(128, dtype=jnp.int32)
    return (lane_ids[None, :] < counts[:, None]).astype(jnp.float32).reshape(-1)

def radiate(obs_position, panel_position, panel_area, spectra, freq_bins):
    offset = obs_position[:, :, None] - panel_position[:, None, :]
    distance = jnp.sqrt(lax.optimization_barrier(jnp.sum(offset * offset, axis=0)))
    inverse = 1.0 / distance
    unit_dir = offset * inverse[None]
    green_scale = panel_area[None, :] * inverse * (1.0 / (4.0 * math.pi))
    freq_count = freq_bins.shape[0]
    real_blocks = spectra[:freq_count].reshape(freq_count // FBLK, FBLK, 4, -1)
    imag_blocks = spectra[freq_count:].reshape(freq_count // FBLK, FBLK, 4, -1)
    bin_blocks = freq_bins.reshape(freq_count // FBLK, FBLK)

    def one_block(block_items):
        real_src, imag_src, bin_block = block_items
        wavenumber = (2.0 * math.pi / (TIME * SPACING) * bin_block.astype(jnp.float32))[:, None, None]
        radial_real = lax.optimization_barrier(jnp.sum(unit_dir[None] * real_src[:, 1:, None, :], axis=1))
        radial_imag = lax.optimization_barrier(jnp.sum(unit_dir[None] * imag_src[:, 1:, None, :], axis=1))
        source_real = -wavenumber * imag_src[:, 0][:, None, :] + radial_real * inverse[None] - wavenumber * radial_imag
        source_imag = wavenumber * real_src[:, 0][:, None, :] + wavenumber * radial_real + radial_imag * inverse[None]
        phase_arg = wavenumber * distance[None]
        cosine = jnp.cos(phase_arg)
        sine_part = jnp.sin(phase_arg)
        out_real = lax.optimization_barrier(jnp.sum(green_scale[None] * (cosine * source_real + sine_part * source_imag), axis=2))
        out_imag = lax.optimization_barrier(jnp.sum(green_scale[None] * (cosine * source_imag - sine_part * source_real), axis=2))
        return jnp.stack([out_real, out_imag])
    result = lax.map(one_block, (real_blocks, imag_blocks, bin_blocks))
    return jnp.transpose(result, (1, 0, 2, 3)).reshape(2, freq_count, -1)

def reference(samples, panel_position, panel_area, panel_counts, obs_position, freq_bins):
    time_rows = jnp.arange(TIME, dtype=jnp.int32)
    window_table = make_table(time_rows, freq_bins)
    flat_samples = samples.reshape(TIME, -1)
    raw_spectra = lax.dot_general(window_table, flat_samples, (((0,), (0,)), ((), ())), preferred_element_type=jnp.float32)
    sources = raw_spectra.reshape(2 * NF, 4, PANELS) * live_rows(panel_counts)[None, None, :]

    def accumulate(running, block_index):
        first_row = block_index * 1024
        slice_spectra = lax.dynamic_slice_in_dim(sources, first_row, 1024, 2)
        block_position = lax.dynamic_slice_in_dim(panel_position, first_row, 1024, 1)
        block_area = lax.dynamic_slice_in_dim(panel_area, first_row, 1024, 0)
        return (running + radiate(obs_position, block_position, block_area, slice_spectra, freq_bins), None)
    running, _ = lax.scan(accumulate, jnp.zeros((2, NF, OBS), jnp.float32), jnp.arange(PANELS // 1024, dtype=jnp.int32))
    return running
```

```python
import math

import jax
import jax.numpy as jnp
from jax import lax
from jax.experimental import pallas as pl
from jax.experimental.pallas import tpu as pltpu
from jax.sharding import PartitionSpec as P

TIME = 1024
NF = 32
FBLK = 4


SPACING = 0.1


def make_table(time_rows, freq_bins):
    phase_index = freq_bins[None, :] * time_rows[:, None] % TIME
    angle_arg = 2.0 * math.pi / TIME * phase_index.astype(jnp.float32)
    window = 0.5 - 0.5 * jnp.cos(2.0 * math.pi / TIME * time_rows.astype(jnp.float32))
    weight = 2.0 / TIME * window[:, None]
    return jnp.concatenate(
        [weight * jnp.cos(angle_arg), -weight * jnp.sin(angle_arg)], axis=1
    ).astype(jnp.bfloat16)


def live_rows(counts):
    lane_ids = jnp.arange(128, dtype=jnp.int32)
    return (lane_ids[None, :] < counts[:, None]).astype(jnp.float32).reshape(-1)


def transform(window_table, turned):
    flat_samples = turned.reshape(window_table.shape[0], -1)
    raw_spectra = lax.dot_general(
        window_table, flat_samples, (((0,), (0,)), ((), ())), preferred_element_type=jnp.float32
    )
    return raw_spectra.reshape(2 * NF, 4, -1)


COS_FIT = (0.9999992221726555, -19.73898256405801, 64.92872767456161, -85.27240653862012, 58.794076313415644, -21.076836027706122)
SIN_FIT = (6.28305579836435, -41.33121428164835, 81.36681479714264, -74.47800123607628, 32.78139377750351)
CHUNK = 16
BLOCK = 128


def horner(fit, x):
    total = jnp.full_like(x, fit[-1])
    for c in fit[-2::-1]:
        total = total * x + c
    return total


def sum_four(x):
    return x + pltpu.roll(x, 1, 0) + pltpu.roll(x, 2, 0) + pltpu.roll(x, 3, 0)


def radiate_core(bins_ref, spec_ref, panel_ref, obs_ref, field_ref, turn_ref, green_ref, inv_ref, wave_ref):
    panels = panel_ref.shape[1]
    obs = obs_ref.shape[1]
    turned = panel_ref[...].T
    ox, oy, oz = obs_ref[0:1, :], obs_ref[1:2, :], obs_ref[2:3, :]
    for p in range(0, panels, CHUNK):
        rows = pl.ds(p, CHUNK)
        part = turned[p : p + CHUNK]
        dx, dy, dz = ox - part[:, 0:1], oy - part[:, 1:2], oz - part[:, 2:3]
        distance = jnp.sqrt(dx * dx + dy * dy + dz * dz)
        inverse = 1.0 / distance
        turn_ref[rows, :] = distance * (1.0 / (TIME * SPACING))
        green_ref[rows, :] = part[:, 3:4] * inverse * (1.0 / (4.0 * math.pi))
        inv_ref[rows, :] = inverse

    row = lax.broadcasted_iota(jnp.int32, (8, panels), 0)
    tail_row = lax.rem(row, 4) == 3
    sign = jnp.where(row < 4, -1.0, 1.0)
    place = jnp.where(tail_row, 0.0, jnp.where(row < 4, panel_ref[...], pltpu.roll(panel_ref[...], 4, 0)))
    live = panel_ref[4:5, :]
    obs_all = obs_ref[...]

    def one_bin(j, carry):
        bin_value = bins_ref[j].astype(jnp.float32)
        wavenumber = bin_value * (2.0 * math.pi / (TIME * SPACING))
        base = spec_ref[pl.ds(pl.multiple_of(j * 8, 8), 8), :] * live
        moment = sum_four(base * place)
        vec = jnp.where(tail_row, -moment, base)
        mono = jnp.where(tail_row, base, 0.0)
        vec_turn = sign * pltpu.roll(vec, 4, 0)
        mono_turn = sign * pltpu.roll(mono, 4, 0)
        coef = [wavenumber * mono_turn, wavenumber * mono, wavenumber * vec_turn, wavenumber * vec, vec, -vec_turn]
        total = jnp.zeros((16, obs), jnp.float32)
        for b in range(0, panels, BLOCK):
            for p in range(b, b + BLOCK, CHUNK):
                rows = pl.ds(p, CHUNK)
                turns = turn_ref[rows, :] * bin_value
                turns = turns - jnp.round(turns)
                square = turns * turns
                green = green_ref[rows, :]
                inverse = inv_ref[rows, :]
                real = horner(COS_FIT, square) * green
                imag = horner(SIN_FIT, square) * (turns * green)
                real1, imag1 = real * inverse, imag * inverse
                for s, w in enumerate((real, imag, real1, imag1, real1 * inverse, imag1 * inverse)):
                    wave_ref[pl.ds(b * 6 + s * BLOCK + p - b, CHUNK), :] = w.astype(jnp.bfloat16)
            left = jnp.concatenate([c[:, b : b + BLOCK] for c in coef], axis=1)
            high = left.astype(jnp.bfloat16)
            low = (left - high.astype(jnp.float32)).astype(jnp.bfloat16)
            total = total + jnp.dot(
                jnp.concatenate([high, low], axis=0),
                wave_ref[pl.ds(b * 6, 6 * BLOCK), :],
                preferred_element_type=jnp.float32,
            )
        both = sum_four((total[:8] + total[8:]) * obs_all)
        field_ref[pl.ds(j, 1), :] = both[3:4]
        field_ref[pl.ds(j + NF, 1), :] = both[7:8]
        return carry

    lax.fori_loop(0, NF, one_bin, 0)


def radiate(obs_position, panel_position, panel_area, live, spectra, freq_bins):
    panels = panel_area.shape[0]
    obs = obs_position.shape[1]
    order = spectra.reshape(2, NF, 4, panels).transpose(1, 0, 2, 3)
    order = jnp.concatenate([order[:, :, 1:], order[:, :, :1]], axis=2).reshape(NF * 8, panels)
    panel_rows = jnp.concatenate([panel_position, panel_area[None], live[None], jnp.zeros((3, panels), jnp.float32)])
    ones = jnp.ones((1, obs), jnp.float32)
    obs_rows = jnp.concatenate([obs_position, ones, obs_position, ones])
    vm = pl.BlockSpec(memory_space=pltpu.VMEM)
    return pl.pallas_call(
        radiate_core,
        out_shape=jax.ShapeDtypeStruct((2 * NF, obs), jnp.float32),
        in_specs=[pl.BlockSpec(memory_space=pltpu.SMEM), vm, vm, vm],
        out_specs=vm,
        scratch_shapes=[
            pltpu.VMEM((panels, obs), jnp.float32),
            pltpu.VMEM((panels, obs), jnp.float32),
            pltpu.VMEM((panels, obs), jnp.float32),
            pltpu.VMEM((panels * 6, obs), jnp.bfloat16),
        ],
        compiler_params=pltpu.CompilerParams(vmem_limit_bytes=32 * 1024 * 1024),
        name="radiate",
    )(freq_bins, order, panel_rows, obs_rows)


def shards(samples, panel_position, panel_area, panel_counts, obs_position, freq_bins):
    slab_len = samples.shape[0]
    panel_count = lax.axis_size("panel")
    obs_count = lax.axis_size("obs")
    source_slabs = jnp.arange(panel_count, dtype=jnp.int32)
    inner_step = jnp.arange(slab_len, dtype=jnp.int32)
    turned = lax.all_to_all(
        lax.all_to_all(samples, "panel", split_axis=2, concat_axis=0, tiled=True),
        "obs",
        split_axis=2,
        concat_axis=0,
        tiled=True,
    )
    quarters = jnp.arange(obs_count, dtype=jnp.int32)
    time_rows = (
        (source_slabs[None, :, None] * obs_count + quarters[:, None, None]) * slab_len
        + inner_step[None, None, :]
    ).reshape(-1)
    local_spectra = transform(make_table(time_rows, freq_bins), turned)
    spectra = lax.all_gather(local_spectra, "obs", axis=2, tiled=True)
    field = radiate(
        obs_position, panel_position, panel_area, live_rows(panel_counts), spectra, freq_bins
    )
    parts = field.T.reshape(panel_count, -1, 2 * NF)
    parts = lax.all_to_all(parts, "panel", split_axis=0, concat_axis=0, tiled=True)
    return jnp.sum(parts, axis=0).T.reshape(2, NF, -1)


def solution(mesh):
    in_specs = (
        P(("panel", "obs"), None, None),
        P(None, "panel"),
        P("panel"),
        P("panel"),
        P(None, "obs"),
        P(),
    )
    out_specs = P(None, None, ("obs", "panel"))
    return jax.shard_map(shards, mesh=mesh, in_specs=in_specs, out_specs=out_specs, check_vma=False)
```

```python
import functools
import math

import jax
import jax.numpy as jnp
from jax import lax
from jax.experimental import pallas as pl
from jax.experimental.pallas import tpu as pltpu
from jax.sharding import PartitionSpec as P

TIME = 1024
NF = 32
FBLK = 4


SPACING = 0.1
MESH = pl.DeviceIdType.MESH


def live_rows(counts):
    lane_ids = jnp.arange(128, dtype=jnp.int32)
    return (lane_ids[None, :] < counts[:, None]).astype(jnp.float32).reshape(-1)


COS_FIT = (0.9999992221726555, -19.73898256405801, 64.92872767456161, -85.27240653862012, 58.794076313415644, -21.076836027706122)
SIN_FIT = (6.28305579836435, -41.33121428164835, 81.36681479714264, -74.47800123607628, 32.78139377750351)
SIN_FINE = (6.283182818550581, -41.34142139830231, 81.59618385833781, -76.5801003424203, 41.20539394682785, -12.271260758957148)
CHUNK = 16
BLOCK = 128


def horner(fit, x):
    total = jnp.full_like(x, fit[-1])
    for c in fit[-2::-1]:
        total = total * x + c
    return total


def sum_four(x):
    return x + pltpu.roll(x, 1, 0) + pltpu.roll(x, 2, 0) + pltpu.roll(x, 3, 0)


def radiate_core(bins_ref, spec_ref, panel_ref, obs_ref, field_ref, turn_ref, green_ref, inv_ref, wave_ref):
    panels = panel_ref.shape[1]
    obs = obs_ref.shape[1]
    turned = panel_ref[...].T
    ox, oy, oz = obs_ref[0:1, :], obs_ref[1:2, :], obs_ref[2:3, :]
    for p in range(0, panels, CHUNK):
        rows = pl.ds(p, CHUNK)
        part = turned[p : p + CHUNK]
        dx, dy, dz = ox - part[:, 0:1], oy - part[:, 1:2], oz - part[:, 2:3]
        distance = jnp.sqrt(dx * dx + dy * dy + dz * dz)
        inverse = 1.0 / distance
        turn_ref[rows, :] = distance * (1.0 / (TIME * SPACING))
        green_ref[rows, :] = part[:, 3:4] * inverse * (1.0 / (4.0 * math.pi))
        inv_ref[rows, :] = inverse

    row = lax.broadcasted_iota(jnp.int32, (8, panels), 0)
    tail_row = lax.rem(row, 4) == 3
    sign = jnp.where(row < 4, -1.0, 1.0)
    place = jnp.where(tail_row, 0.0, jnp.where(row < 4, panel_ref[...], pltpu.roll(panel_ref[...], 4, 0)))
    live = panel_ref[4:5, :]
    obs_all = obs_ref[...]

    def one_bin(j, carry):
        bin_value = bins_ref[j].astype(jnp.float32)
        wavenumber = bin_value * (2.0 * math.pi / (TIME * SPACING))
        rows_of_bin = pl.ds(pl.multiple_of(j * 8, 8), 8)
        base = jnp.concatenate([spec_ref[q, rows_of_bin, :] for q in range(spec_ref.shape[0])], axis=1) * live
        moment = sum_four(base * place)
        vec = jnp.where(tail_row, -moment, base)
        mono = jnp.where(tail_row, base, 0.0)
        vec_turn = sign * pltpu.roll(vec, 4, 0)
        mono_turn = sign * pltpu.roll(mono, 4, 0)
        coef = [wavenumber * mono_turn, wavenumber * mono, wavenumber * vec_turn, wavenumber * vec, vec, -vec_turn]
        total = jnp.zeros((16, obs), jnp.float32)
        for b in range(0, panels, BLOCK):
            for p in range(b, b + BLOCK, CHUNK):
                rows = pl.ds(p, CHUNK)
                turns = turn_ref[rows, :] * bin_value
                turns = turns - jnp.round(turns)
                square = turns * turns
                green = green_ref[rows, :]
                inverse = inv_ref[rows, :]
                real = horner(COS_FIT, square) * green
                imag = horner(SIN_FIT, square) * (turns * green)
                real1, imag1 = real * inverse, imag * inverse
                for s, w in enumerate((real, imag, real1, imag1, real1 * inverse, imag1 * inverse)):
                    wave_ref[pl.ds(b * 6 + s * BLOCK + p - b, CHUNK), :] = w.astype(jnp.bfloat16)
            left = jnp.concatenate([c[:, b : b + BLOCK] for c in coef], axis=1)
            high = left.astype(jnp.bfloat16)
            low = (left - high.astype(jnp.float32)).astype(jnp.bfloat16)
            total = total + jnp.dot(
                jnp.concatenate([high, low], axis=0),
                wave_ref[pl.ds(b * 6, 6 * BLOCK), :],
                preferred_element_type=jnp.float32,
            )
        both = sum_four((total[:8] + total[8:]) * obs_all)
        field_ref[pl.ds(j, 1), :] = both[3:4]
        field_ref[pl.ds(j + NF, 1), :] = both[7:8]
        return carry

    lax.fori_loop(0, NF, one_bin, 0)


def radiate(obs_position, panel_position, panel_area, live, spectra, freq_bins):
    panels = panel_area.shape[0]
    obs = obs_position.shape[1]
    panel_rows = jnp.concatenate([panel_position, panel_area[None], live[None], jnp.zeros((3, panels), jnp.float32)])
    ones = jnp.ones((1, obs), jnp.float32)
    obs_rows = jnp.concatenate([obs_position, ones, obs_position, ones])
    vm = pl.BlockSpec(memory_space=pltpu.VMEM)
    return pl.pallas_call(
        radiate_core,
        out_shape=jax.ShapeDtypeStruct((2 * NF, obs), jnp.float32),
        in_specs=[pl.BlockSpec(memory_space=pltpu.SMEM), vm, vm, vm],
        out_specs=vm,
        scratch_shapes=[
            pltpu.VMEM((panels, obs), jnp.float32),
            pltpu.VMEM((panels, obs), jnp.float32),
            pltpu.VMEM((panels, obs), jnp.float32),
            pltpu.VMEM((panels * 6, obs), jnp.bfloat16),
        ],
        compiler_params=pltpu.CompilerParams(vmem_limit_bytes=32 * 1024 * 1024),
        name="radiate",
    )(freq_bins, spectra, panel_rows, obs_rows)


def spectra_table(bin_rows, first_time, depth):
    rows = bin_rows.shape[0]
    row = lax.broadcasted_iota(jnp.int32, (rows, depth), 0)
    column = lax.broadcasted_iota(jnp.int32, (rows, depth), 1)
    time = first_time + (column >> 2)
    index = (bin_rows * time) & (TIME - 1)
    turns = index.astype(jnp.float32) * (1.0 / TIME)
    turns = turns - jnp.round(turns)
    real = horner(COS_FIT, turns * turns)
    imag = -horner(SIN_FINE, turns * turns) * turns
    window_turns = time.astype(jnp.float32) * (1.0 / TIME)
    window_turns = window_turns - jnp.round(window_turns)
    window = 0.5 - 0.5 * horner(COS_FIT, window_turns * window_turns)
    weight = 2.0 / TIME * window
    value = weight * jnp.where((row & 4) == 0, real, imag)
    return jnp.where((row & 3) == ((column + 3) & 3), value, 0.0).astype(jnp.bfloat16)


def spectra_kernel(
    groups, width, samples_ref, bins_ref, out_ref, table, held, mine, send, arrived,
    own_sem, sample_send, sample_recv, part_send, part_recv, sum_send, sum_recv,
):
    panel_count, obs_count = groups
    panel, obs = lax.axis_index("panel"), lax.axis_index("obs")
    slab = samples_ref.shape[0]
    block = width * obs_count

    barrier = pltpu.get_barrier_semaphore()
    for k in range(1, obs_count):
        pl.semaphore_signal(barrier, inc=1, device_id=(panel, lax.rem(obs + k, obs_count)), device_id_type=MESH)

    def greet(k, carry):
        pl.semaphore_signal(barrier, inc=1, device_id=(lax.rem(panel + k, panel_count), obs), device_id_type=MESH)
        return carry

    lax.fori_loop(1, panel_count, greet, 0)

    def piece(step, part):
        first = lax.rem(panel + 1 + step, panel_count) * block + part * width
        return samples_ref.at[:, :, pl.ds(pl.multiple_of(first, 128), width)]

    def own_copy(step):
        return pltpu.make_async_copy(piece(step, obs), held.at[step, obs], own_sem.at[step])

    def sample_copy(step, k):
        other = lax.rem(obs + k, obs_count)
        return pltpu.make_async_remote_copy(
            src_ref=piece(step, other),
            dst_ref=held.at[step, obs],
            send_sem=sample_send.at[k - 1, step],
            recv_sem=sample_recv.at[k - 1, step],
            device_id=(panel, other),
            device_id_type=MESH,
        )

    def part_copy(step):
        return pltpu.make_async_remote_copy(
            src_ref=send.at[step],
            dst_ref=arrived.at[step],
            send_sem=part_send.at[step],
            recv_sem=part_recv.at[step],
            device_id=(lax.rem(panel + 1 + step, panel_count), obs),
            device_id_type=MESH,
        )

    def sum_copy(k):
        return pltpu.make_async_remote_copy(
            src_ref=out_ref.at[obs],
            dst_ref=out_ref.at[obs],
            send_sem=sum_send.at[k - 1],
            recv_sem=sum_recv.at[k - 1],
            device_id=(panel, lax.rem(obs + k, obs_count)),
            device_id_type=MESH,
        )

    pl.semaphore_wait(barrier, obs_count + panel_count - 2)

    def launch(step, carry):
        for k in range(1, obs_count):
            sample_copy(step, k).start()
        own_copy(step).start()
        return carry

    lax.fori_loop(0, panel_count, launch, 0)
    table[...] = spectra_table(bins_ref[...], panel * obs_count * slab, table.shape[1])

    def transform(step):
        own_copy(step).wait()
        for k in range(1, obs_count):
            sample_copy(step, k).wait_recv()
        return jnp.dot(
            table[...], held[step].reshape(table.shape[1], width), preferred_element_type=jnp.float32
        )

    def one_step(step, carry):
        send[step] = transform(step).astype(jnp.bfloat16)
        part_copy(step).start()
        return carry

    lax.fori_loop(0, panel_count - 1, one_step, 0)
    mine[...] = transform(panel_count - 1)

    def add(step, carry):
        part_copy(step).wait_recv()
        mine[...] += arrived[step].astype(jnp.float32)
        return carry

    lax.fori_loop(0, panel_count - 1, add, 0)
    out_ref[obs] = mine[...]
    for k in range(1, obs_count):
        sum_copy(k).start()
    for k in range(1, obs_count):
        sum_copy(k).wait_recv()

    def drain(step, carry):
        for k in range(1, obs_count):
            sample_copy(step, k).wait_send()
        return carry

    lax.fori_loop(0, panel_count, drain, 0)

    def drain_parts(step, carry):
        part_copy(step).wait_send()
        return carry

    lax.fori_loop(0, panel_count - 1, drain_parts, 0)
    for k in range(1, obs_count):
        sum_copy(k).wait_send()


def all_spectra(samples, freq_bins, panel_count, obs_count):
    slab, channels, panels = samples.shape
    width = panels // (panel_count * obs_count)
    rows = 2 * NF * channels
    depth = slab * channels * obs_count
    bin_rows = jnp.repeat(freq_bins, 2 * channels)[:, None]
    dma = pltpu.SemaphoreType.DMA
    return pl.pallas_call(
        functools.partial(spectra_kernel, (panel_count, obs_count), width),
        out_shape=jax.ShapeDtypeStruct((obs_count, rows, width), jnp.float32),
        in_specs=[pl.BlockSpec(memory_space=pl.ANY), pl.BlockSpec(memory_space=pltpu.VMEM)],
        out_specs=pl.BlockSpec(memory_space=pltpu.VMEM),
        scratch_shapes=[
            pltpu.VMEM((rows, depth), jnp.bfloat16),
            pltpu.VMEM((panel_count, obs_count, slab, channels, width), jnp.bfloat16),
            pltpu.VMEM((rows, width), jnp.float32),
            pltpu.VMEM((panel_count - 1, rows, width), jnp.bfloat16),
            pltpu.VMEM((panel_count - 1, rows, width), jnp.bfloat16),
            dma((panel_count,)),
            dma((obs_count - 1, panel_count)),
            dma((obs_count - 1, panel_count)),
            dma((panel_count - 1,)),
            dma((panel_count - 1,)),
            dma((obs_count - 1,)),
            dma((obs_count - 1,)),
        ],
        compiler_params=pltpu.CompilerParams(
            collective_id=0, has_side_effects=True, vmem_limit_bytes=40 * 1024 * 1024
        ),
        name="spectra",
    )(samples, bin_rows)


def shards(samples, panel_position, panel_area, panel_counts, obs_position, freq_bins):
    panel_count = lax.axis_size("panel")
    obs_count = lax.axis_size("obs")
    spectra = all_spectra(samples, freq_bins, panel_count, obs_count)
    field = radiate(
        obs_position, panel_position, panel_area, live_rows(panel_counts), spectra, freq_bins
    )
    parts = field.T.reshape(panel_count, -1, 2 * NF)
    parts = lax.all_to_all(parts, "panel", split_axis=0, concat_axis=0, tiled=True)
    return jnp.sum(parts, axis=0).T.reshape(2, NF, -1)


def solution(mesh):
    in_specs = (
        P(("panel", "obs"), None, None),
        P(None, "panel"),
        P("panel"),
        P("panel"),
        P(None, "obs"),
        P(),
    )
    out_specs = P(None, None, ("obs", "panel"))
    return jax.shard_map(shards, mesh=mesh, in_specs=in_specs, out_specs=out_specs, check_vma=False)
```

```python
import functools
import math

import jax
import jax.numpy as jnp
from jax import lax
from jax.experimental import pallas as pl
from jax.experimental.pallas import tpu as pltpu
from jax.sharding import PartitionSpec as P

TIME = 1024
NF = 32
FBLK = 4


SPACING = 0.1
MESH = pl.DeviceIdType.MESH


def live_rows(counts):
    lane_ids = jnp.arange(128, dtype=jnp.int32)
    return (lane_ids[None, :] < counts[:, None]).astype(jnp.float32).reshape(-1)


COS_FIT = (0.9999992221726555, -19.73898256405801, 64.92872767456161, -85.27240653862012, 58.794076313415644, -21.076836027706122)
SIN_FIT = (6.28305579836435, -41.33121428164835, 81.36681479714264, -74.47800123607628, 32.78139377750351)
SIN_FINE = (6.283182818550581, -41.34142139830231, 81.59618385833781, -76.5801003424203, 41.20539394682785, -12.271260758957148)
CHUNK = 16
BLOCK = 128


def horner(fit, x):
    total = jnp.full_like(x, fit[-1])
    for c in fit[-2::-1]:
        total = total * x + c
    return total


def sum_four(x):
    return x + pltpu.roll(x, 1, 0) + pltpu.roll(x, 2, 0) + pltpu.roll(x, 3, 0)


def radiate_core(bins_ref, spec_ref, panel_ref, obs_ref, field_ref, turn_ref, green_ref, inv_ref, wave_ref):
    panels = panel_ref.shape[1]
    obs = obs_ref.shape[1]
    turned = panel_ref[...].T
    ox, oy, oz = obs_ref[0:1, :], obs_ref[1:2, :], obs_ref[2:3, :]
    for p in range(0, panels, CHUNK):
        rows = pl.ds(p, CHUNK)
        part = turned[p : p + CHUNK]
        dx, dy, dz = ox - part[:, 0:1], oy - part[:, 1:2], oz - part[:, 2:3]
        distance = jnp.sqrt(dx * dx + dy * dy + dz * dz)
        inverse = 1.0 / distance
        turn_ref[rows, :] = distance * (1.0 / (TIME * SPACING))
        green_ref[rows, :] = part[:, 3:4] * inverse * (1.0 / (4.0 * math.pi))
        inv_ref[rows, :] = inverse

    row = lax.broadcasted_iota(jnp.int32, (8, panels), 0)
    tail_row = lax.rem(row, 4) == 3
    sign = jnp.where(row < 4, -1.0, 1.0)
    place = jnp.where(tail_row, 0.0, jnp.where(row < 4, panel_ref[...], pltpu.roll(panel_ref[...], 4, 0)))
    live = panel_ref[4:5, :]
    obs_all = obs_ref[...]

    def one_bin(j, carry):
        bin_value = bins_ref[j].astype(jnp.float32)
        wavenumber = bin_value * (2.0 * math.pi / (TIME * SPACING))
        rows_of_bin = pl.ds(pl.multiple_of(j * 8, 8), 8)
        base = jnp.concatenate([spec_ref[q, rows_of_bin, :] for q in range(spec_ref.shape[0])], axis=1) * live
        moment = sum_four(base * place)
        vec = jnp.where(tail_row, -moment, base)
        mono = jnp.where(tail_row, base, 0.0)
        vec_turn = sign * pltpu.roll(vec, 4, 0)
        mono_turn = sign * pltpu.roll(mono, 4, 0)
        coef = [wavenumber * mono_turn, wavenumber * mono, wavenumber * vec_turn, wavenumber * vec, vec, -vec_turn]
        total = jnp.zeros((16, obs), jnp.float32)
        for b in range(0, panels, BLOCK):
            for p in range(b, b + BLOCK, CHUNK):
                rows = pl.ds(p, CHUNK)
                turns = turn_ref[rows, :] * bin_value
                turns = turns - jnp.round(turns)
                square = turns * turns
                green = green_ref[rows, :]
                inverse = inv_ref[rows, :]
                real = horner(COS_FIT, square) * green
                imag = horner(SIN_FIT, square) * (turns * green)
                real1, imag1 = real * inverse, imag * inverse
                for s, w in enumerate((real, imag, real1, imag1, real1 * inverse, imag1 * inverse)):
                    wave_ref[pl.ds(b * 6 + s * BLOCK + p - b, CHUNK), :] = w.astype(jnp.bfloat16)
            left = jnp.concatenate([c[:, b : b + BLOCK] for c in coef], axis=1)
            high = left.astype(jnp.bfloat16)
            low = (left - high.astype(jnp.float32)).astype(jnp.bfloat16)
            total = total + jnp.dot(
                jnp.concatenate([high, low], axis=0),
                wave_ref[pl.ds(b * 6, 6 * BLOCK), :],
                preferred_element_type=jnp.float32,
            )
        both = sum_four((total[:8] + total[8:]) * obs_all)
        field_ref[pl.ds(j, 1), :] = both[3:4]
        field_ref[pl.ds(j + NF, 1), :] = both[7:8]
        return carry

    lax.fori_loop(0, NF, one_bin, 0)


def radiate(obs_position, panel_position, panel_area, live, spectra, freq_bins):
    panels = panel_area.shape[0]
    obs = obs_position.shape[1]
    panel_rows = jnp.concatenate([panel_position, panel_area[None], live[None], jnp.zeros((3, panels), jnp.float32)])
    ones = jnp.ones((1, obs), jnp.float32)
    obs_rows = jnp.concatenate([obs_position, ones, obs_position, ones])
    vm = pl.BlockSpec(memory_space=pltpu.VMEM)
    return pl.pallas_call(
        radiate_core,
        out_shape=jax.ShapeDtypeStruct((2 * NF, obs), jnp.float32),
        in_specs=[pl.BlockSpec(memory_space=pltpu.SMEM), vm, vm, vm],
        out_specs=vm,
        scratch_shapes=[
            pltpu.VMEM((panels, obs), jnp.float32),
            pltpu.VMEM((panels, obs), jnp.float32),
            pltpu.VMEM((panels, obs), jnp.float32),
            pltpu.VMEM((panels * 6, obs), jnp.bfloat16),
        ],
        compiler_params=pltpu.CompilerParams(vmem_limit_bytes=32 * 1024 * 1024),
        name="radiate",
    )(freq_bins, spectra, panel_rows, obs_rows)


def spectra_table(first_bin, second_bin, first_time, depth):
    row = lax.broadcasted_iota(jnp.int32, (16, depth), 0)
    column = lax.broadcasted_iota(jnp.int32, (16, depth), 1)
    time = first_time + (column >> 2)
    index = (jnp.where(row < 8, first_bin, second_bin) * time) & (TIME - 1)
    turns = index.astype(jnp.float32) * (1.0 / TIME)
    turns = turns - jnp.round(turns)
    real = horner(COS_FIT, turns * turns)
    imag = -horner(SIN_FINE, turns * turns) * turns
    window_turns = time.astype(jnp.float32) * (1.0 / TIME)
    window_turns = window_turns - jnp.round(window_turns)
    window = 0.5 - 0.5 * horner(COS_FIT, window_turns * window_turns)
    weight = 2.0 / TIME * window
    value = weight * jnp.where((row & 4) == 0, real, imag)
    return jnp.where((row & 3) == ((column + 3) & 3), value, 0.0).astype(jnp.bfloat16)


def spectra_kernel(
    groups, width, samples_ref, bins_ref, out_ref, table, held, mine, send, arrived,
    own_sem, sample_send, sample_recv, part_send, part_recv, sum_send, sum_recv,
):
    panel_count, obs_count = groups
    panel, obs = lax.axis_index("panel"), lax.axis_index("obs")
    slab = samples_ref.shape[0]
    block = width * obs_count

    barrier = pltpu.get_barrier_semaphore()
    for k in range(1, obs_count):
        pl.semaphore_signal(barrier, inc=1, device_id=(panel, lax.rem(obs + k, obs_count)), device_id_type=MESH)

    def greet(k, carry):
        pl.semaphore_signal(barrier, inc=1, device_id=(lax.rem(panel + k, panel_count), obs), device_id_type=MESH)
        return carry

    lax.fori_loop(1, panel_count, greet, 0)

    def piece(step, part):
        first = lax.rem(panel + 1 + step, panel_count) * block + part * width
        return samples_ref.at[:, :, pl.ds(pl.multiple_of(first, 128), width)]

    def own_copy(step):
        return pltpu.make_async_copy(piece(step, obs), held.at[step, obs], own_sem.at[step])

    def sample_copy(step, k):
        other = lax.rem(obs + k, obs_count)
        return pltpu.make_async_remote_copy(
            src_ref=piece(step, other),
            dst_ref=held.at[step, obs],
            send_sem=sample_send.at[k - 1, step],
            recv_sem=sample_recv.at[k - 1, step],
            device_id=(panel, other),
            device_id_type=MESH,
        )

    def part_copy(step):
        return pltpu.make_async_remote_copy(
            src_ref=send.at[step],
            dst_ref=arrived.at[step],
            send_sem=part_send.at[step],
            recv_sem=part_recv.at[step],
            device_id=(lax.rem(panel + 1 + step, panel_count), obs),
            device_id_type=MESH,
        )

    def sum_copy(k):
        return pltpu.make_async_remote_copy(
            src_ref=out_ref.at[obs],
            dst_ref=out_ref.at[obs],
            send_sem=sum_send.at[k - 1],
            recv_sem=sum_recv.at[k - 1],
            device_id=(panel, lax.rem(obs + k, obs_count)),
            device_id_type=MESH,
        )

    pl.semaphore_wait(barrier, obs_count + panel_count - 2)

    def launch(step, carry):
        for k in range(1, obs_count):
            sample_copy(step, k).start()
        own_copy(step).start()
        return carry

    lax.fori_loop(0, panel_count, launch, 0)
    first_time = panel * obs_count * slab

    def two_bins(i, carry):
        table[pl.ds(pl.multiple_of(i * 16, 16), 16), :] = spectra_table(
            bins_ref[2 * i], bins_ref[2 * i + 1], first_time, table.shape[1]
        )
        return carry

    lax.fori_loop(0, NF // 2, two_bins, 0)

    def transform(step):
        own_copy(step).wait()
        for k in range(1, obs_count):
            sample_copy(step, k).wait_recv()
        return jnp.dot(
            table[...], held[step].reshape(table.shape[1], width), preferred_element_type=jnp.float32
        )

    def one_step(step, carry):
        send[step] = transform(step).astype(jnp.bfloat16)
        part_copy(step).start()
        return carry

    lax.fori_loop(0, panel_count - 1, one_step, 0)
    mine[...] = transform(panel_count - 1)

    def add(step, carry):
        part_copy(step).wait_recv()
        mine[...] += arrived[step].astype(jnp.float32)
        return carry

    lax.fori_loop(0, panel_count - 1, add, 0)
    out_ref[obs] = mine[...]
    for k in range(1, obs_count):
        sum_copy(k).start()
    for k in range(1, obs_count):
        sum_copy(k).wait_recv()

    def drain(step, carry):
        for k in range(1, obs_count):
            sample_copy(step, k).wait_send()
        return carry

    lax.fori_loop(0, panel_count, drain, 0)

    def drain_parts(step, carry):
        part_copy(step).wait_send()
        return carry

    lax.fori_loop(0, panel_count - 1, drain_parts, 0)
    for k in range(1, obs_count):
        sum_copy(k).wait_send()


def all_spectra(samples, freq_bins, panel_count, obs_count):
    slab, channels, panels = samples.shape
    width = panels // (panel_count * obs_count)
    rows = 2 * NF * channels
    depth = slab * channels * obs_count
    dma = pltpu.SemaphoreType.DMA
    return pl.pallas_call(
        functools.partial(spectra_kernel, (panel_count, obs_count), width),
        out_shape=jax.ShapeDtypeStruct((obs_count, rows, width), jnp.float32),
        in_specs=[pl.BlockSpec(memory_space=pl.ANY), pl.BlockSpec(memory_space=pltpu.SMEM)],
        out_specs=pl.BlockSpec(memory_space=pltpu.VMEM),
        scratch_shapes=[
            pltpu.VMEM((rows, depth), jnp.bfloat16),
            pltpu.VMEM((panel_count, obs_count, slab, channels, width), jnp.bfloat16),
            pltpu.VMEM((rows, width), jnp.float32),
            pltpu.VMEM((panel_count - 1, rows, width), jnp.bfloat16),
            pltpu.VMEM((panel_count - 1, rows, width), jnp.bfloat16),
            dma((panel_count,)),
            dma((obs_count - 1, panel_count)),
            dma((obs_count - 1, panel_count)),
            dma((panel_count - 1,)),
            dma((panel_count - 1,)),
            dma((obs_count - 1,)),
            dma((obs_count - 1,)),
        ],
        compiler_params=pltpu.CompilerParams(
            collective_id=0, has_side_effects=True, vmem_limit_bytes=40 * 1024 * 1024
        ),
        name="spectra",
    )(samples, freq_bins)


def collect_kernel(panel_count, field_ref, out_ref, staged, arrived, send_sem, recv_sem):
    panel, obs = lax.axis_index("panel"), lax.axis_index("obs")
    rows = staged.shape[1]

    barrier = pltpu.get_barrier_semaphore()

    def greet(k, carry):
        pl.semaphore_signal(barrier, inc=1, device_id=(lax.rem(panel + k, panel_count), obs), device_id_type=MESH)
        return carry

    lax.fori_loop(1, panel_count, greet, 0)
    field = field_ref[...]
    turned = jnp.concatenate([field, jnp.zeros((128 - field.shape[0], field.shape[1]), jnp.float32)], axis=0).T
    for b in range(panel_count):
        staged[b] = turned[b * rows : (b + 1) * rows]

    def copy(k):
        other = lax.rem(panel + k, panel_count)
        return pltpu.make_async_remote_copy(
            src_ref=staged.at[other],
            dst_ref=arrived.at[k - 1],
            send_sem=send_sem.at[k - 1],
            recv_sem=recv_sem.at[k - 1],
            device_id=(other, obs),
            device_id_type=MESH,
        )

    pl.semaphore_wait(barrier, panel_count - 1)

    def launch(k, carry):
        copy(k).start()
        return carry

    lax.fori_loop(1, panel_count, launch, 0)

    def add(k, total):
        copy(k).wait_recv()
        return total + arrived[k - 1]

    total = lax.fori_loop(1, panel_count, add, staged[panel])
    out_ref[...] = total

    def drain(k, carry):
        copy(k).wait_send()
        return carry

    lax.fori_loop(1, panel_count, drain, 0)


def collect(field, panel_count):
    rows = field.shape[1] // panel_count
    dma = pltpu.SemaphoreType.DMA
    vm = pl.BlockSpec(memory_space=pltpu.VMEM)
    return pl.pallas_call(
        functools.partial(collect_kernel, panel_count),
        out_shape=jax.ShapeDtypeStruct((rows, 128), jnp.float32),
        in_specs=[vm],
        out_specs=vm,
        scratch_shapes=[
            pltpu.VMEM((panel_count, rows, 128), jnp.float32),
            pltpu.VMEM((panel_count - 1, rows, 128), jnp.float32),
            dma((panel_count - 1,)),
            dma((panel_count - 1,)),
        ],
        compiler_params=pltpu.CompilerParams(
            collective_id=1, has_side_effects=True, vmem_limit_bytes=16 * 1024 * 1024
        ),
        name="collect",
    )(field)


def shards(samples, panel_position, panel_area, panel_counts, obs_position, freq_bins):
    panel_count = lax.axis_size("panel")
    obs_count = lax.axis_size("obs")
    spectra = all_spectra(samples, freq_bins, panel_count, obs_count)
    field = radiate(
        obs_position, panel_position, panel_area, live_rows(panel_counts), spectra, freq_bins
    )
    total = collect(field, panel_count)[:, : 2 * NF]
    return total.T.reshape(2, NF, -1)


def solution(mesh):
    in_specs = (
        P(("panel", "obs"), None, None),
        P(None, "panel"),
        P("panel"),
        P("panel"),
        P(None, "obs"),
        P(),
    )
    out_specs = P(None, None, ("obs", "panel"))
    return jax.shard_map(shards, mesh=mesh, in_specs=in_specs, out_specs=out_specs, check_vma=False)
```

```python
import functools
import math

import jax
import jax.numpy as jnp
from jax import lax
from jax.experimental import pallas as pl
from jax.experimental.pallas import tpu as pltpu
from jax.sharding import PartitionSpec as P

TIME = 1024
NF = 32
FBLK = 4


SPACING = 0.1
MESH = pl.DeviceIdType.MESH


def live_rows(counts):
    lane_ids = jnp.arange(128, dtype=jnp.int32)
    return (lane_ids[None, :] < counts[:, None]).astype(jnp.float32).reshape(-1)


COS_FIT = (0.9999992221726555, -19.73898256405801, 64.92872767456161, -85.27240653862012, 58.794076313415644, -21.076836027706122)
SIN_FIT = (6.28305579836435, -41.33121428164835, 81.36681479714264, -74.47800123607628, 32.78139377750351)
SIN_FINE = (6.283182818550581, -41.34142139830231, 81.59618385833781, -76.5801003424203, 41.20539394682785, -12.271260758957148)
CHUNK = 16
BLOCK = 128


def horner(fit, x):
    total = jnp.full_like(x, fit[-1])
    for c in fit[-2::-1]:
        total = total * x + c
    return total


def sum_four(x):
    return x + pltpu.roll(x, 1, 0) + pltpu.roll(x, 2, 0) + pltpu.roll(x, 3, 0)


def radiate_core(bins_ref, spec_ref, panel_ref, obs_ref, field_ref, turn_ref, green_ref, inv_ref, short_ref, wave_ref):
    panels = panel_ref.shape[1]
    obs = obs_ref.shape[1]
    turned = panel_ref[...].T
    ox, oy, oz = obs_ref[0:1, :], obs_ref[1:2, :], obs_ref[2:3, :]
    for p in range(0, panels, CHUNK):
        rows = pl.ds(p, CHUNK)
        part = turned[p : p + CHUNK]
        dx, dy, dz = ox - part[:, 0:1], oy - part[:, 1:2], oz - part[:, 2:3]
        distance = jnp.sqrt(dx * dx + dy * dy + dz * dz)
        inverse = 1.0 / distance
        turn_ref[rows, :] = distance * (1.0 / (TIME * SPACING))
        green_ref[rows, :] = part[:, 3:4] * inverse * (1.0 / (4.0 * math.pi))
        inv_ref[rows, :] = inverse
        short_ref[rows, :] = inverse.astype(jnp.bfloat16)

    row = lax.broadcasted_iota(jnp.int32, (8, panels), 0)
    tail_row = lax.rem(row, 4) == 3
    sign = jnp.where(row < 4, -1.0, 1.0)
    place = jnp.where(tail_row, 0.0, jnp.where(row < 4, panel_ref[...], pltpu.roll(panel_ref[...], 4, 0)))
    live = panel_ref[4:5, :]
    obs_all = obs_ref[...]

    def one_bin(j, slot):
        bin_value = bins_ref[j].astype(jnp.float32)
        wavenumber = bin_value * (2.0 * math.pi / (TIME * SPACING))
        rows_of_bin = pl.ds(pl.multiple_of(j * 8, 8), 8)
        base = jnp.concatenate([spec_ref[q, rows_of_bin, :] for q in range(spec_ref.shape[0])], axis=1) * live
        moment = sum_four(base * place)
        vec = jnp.where(tail_row, -moment, base)
        mono = jnp.where(tail_row, base, 0.0)
        vec_turn = sign * pltpu.roll(vec, 4, 0)
        mono_turn = sign * pltpu.roll(mono, 4, 0)
        coef = [wavenumber * mono_turn, wavenumber * mono, wavenumber * vec_turn, wavenumber * vec, vec, -vec_turn]
        total = jnp.zeros((16, obs), jnp.float32)
        for b in range(0, panels, BLOCK):
            for p in range(b, b + BLOCK, CHUNK):
                rows = pl.ds(p, CHUNK)
                turns = turn_ref[rows, :] * bin_value
                turns = turns - jnp.round(turns)
                square = turns * turns
                green = green_ref[rows, :]
                inverse = inv_ref[rows, :]
                real = horner(COS_FIT, square) * green
                imag = horner(SIN_FIT, square) * (turns * green)
                real1, imag1 = real * inverse, imag * inverse
                waves = [w.astype(jnp.bfloat16) for w in (real, imag, real1, imag1)]
                short = short_ref[rows, :]
                waves += [waves[2] * short, waves[3] * short]
                for s, w in enumerate(waves):
                    wave_ref[slot, pl.ds(b * 6 + s * BLOCK + p - b, CHUNK), :] = w
            left = jnp.concatenate([c[:, b : b + BLOCK] for c in coef], axis=1)
            high = left.astype(jnp.bfloat16)
            low = (left - high.astype(jnp.float32)).astype(jnp.bfloat16)
            total = total + jnp.dot(
                jnp.concatenate([high, low], axis=0),
                wave_ref[slot, pl.ds(b * 6, 6 * BLOCK), :],
                preferred_element_type=jnp.float32,
            )
        both = sum_four((total[:8] + total[8:]) * obs_all)
        field_ref[pl.ds(j, 1), :] = both[3:4]
        field_ref[pl.ds(j + NF, 1), :] = both[7:8]

    def two_bins(i, carry):
        one_bin(2 * i, 0)
        one_bin(2 * i + 1, 1)
        return carry

    lax.fori_loop(0, NF // 2, two_bins, 0)


def radiate(obs_position, panel_position, panel_area, live, spectra, freq_bins):
    panels = panel_area.shape[0]
    obs = obs_position.shape[1]
    panel_rows = jnp.concatenate([panel_position, panel_area[None], live[None], jnp.zeros((3, panels), jnp.float32)])
    ones = jnp.ones((1, obs), jnp.float32)
    obs_rows = jnp.concatenate([obs_position, ones, obs_position, ones])
    vm = pl.BlockSpec(memory_space=pltpu.VMEM)
    return pl.pallas_call(
        radiate_core,
        out_shape=jax.ShapeDtypeStruct((2 * NF, obs), jnp.float32),
        in_specs=[pl.BlockSpec(memory_space=pltpu.SMEM), vm, vm, vm],
        out_specs=vm,
        scratch_shapes=[
            pltpu.VMEM((panels, obs), jnp.float32),
            pltpu.VMEM((panels, obs), jnp.float32),
            pltpu.VMEM((panels, obs), jnp.float32),
            pltpu.VMEM((panels, obs), jnp.bfloat16),
            pltpu.VMEM((2, panels * 6, obs), jnp.bfloat16),
        ],
        compiler_params=pltpu.CompilerParams(vmem_limit_bytes=32 * 1024 * 1024),
        name="radiate",
    )(freq_bins, spectra, panel_rows, obs_rows)


def spectra_table(first_bin, second_bin, first_time, depth):
    row = lax.broadcasted_iota(jnp.int32, (16, depth), 0)
    column = lax.broadcasted_iota(jnp.int32, (16, depth), 1)
    time = first_time + (column >> 2)
    index = (jnp.where(row < 8, first_bin, second_bin) * time) & (TIME - 1)
    turns = index.astype(jnp.float32) * (1.0 / TIME)
    turns = turns - jnp.round(turns)
    real = horner(COS_FIT, turns * turns)
    imag = -horner(SIN_FINE, turns * turns) * turns
    window_turns = time.astype(jnp.float32) * (1.0 / TIME)
    window_turns = window_turns - jnp.round(window_turns)
    window = 0.5 - 0.5 * horner(COS_FIT, window_turns * window_turns)
    weight = 2.0 / TIME * window
    value = weight * jnp.where((row & 4) == 0, real, imag)
    return jnp.where((row & 3) == ((column + 3) & 3), value, 0.0).astype(jnp.bfloat16)


def spectra_kernel(
    groups, width, samples_ref, bins_ref, out_ref, table, held, mine, send, arrived,
    own_sem, sample_send, sample_recv, part_send, part_recv, sum_send, sum_recv,
):
    panel_count, obs_count = groups
    panel, obs = lax.axis_index("panel"), lax.axis_index("obs")
    slab = samples_ref.shape[0]
    block = width * obs_count

    barrier = pltpu.get_barrier_semaphore()
    for k in range(1, obs_count):
        pl.semaphore_signal(barrier, inc=1, device_id=(panel, lax.rem(obs + k, obs_count)), device_id_type=MESH)

    def greet(k, carry):
        pl.semaphore_signal(barrier, inc=1, device_id=(lax.rem(panel + k, panel_count), obs), device_id_type=MESH)
        return carry

    lax.fori_loop(1, panel_count, greet, 0)

    def piece(step, part):
        first = lax.rem(panel + 1 + step, panel_count) * block + part * width
        return samples_ref.at[:, :, pl.ds(pl.multiple_of(first, 128), width)]

    def own_copy(step):
        return pltpu.make_async_copy(piece(step, obs), held.at[step, obs], own_sem.at[step])

    def sample_copy(step, k):
        other = lax.rem(obs + k, obs_count)
        return pltpu.make_async_remote_copy(
            src_ref=piece(step, other),
            dst_ref=held.at[step, obs],
            send_sem=sample_send.at[k - 1, step],
            recv_sem=sample_recv.at[k - 1, step],
            device_id=(panel, other),
            device_id_type=MESH,
        )

    def part_copy(step):
        return pltpu.make_async_remote_copy(
            src_ref=send.at[step],
            dst_ref=arrived.at[step],
            send_sem=part_send.at[step],
            recv_sem=part_recv.at[step],
            device_id=(lax.rem(panel + 1 + step, panel_count), obs),
            device_id_type=MESH,
        )

    def sum_copy(k):
        return pltpu.make_async_remote_copy(
            src_ref=out_ref.at[obs],
            dst_ref=out_ref.at[obs],
            send_sem=sum_send.at[k - 1],
            recv_sem=sum_recv.at[k - 1],
            device_id=(panel, lax.rem(obs + k, obs_count)),
            device_id_type=MESH,
        )

    pl.semaphore_wait(barrier, obs_count + panel_count - 2)

    def launch(step, carry):
        for k in range(1, obs_count):
            sample_copy(step, k).start()
        own_copy(step).start()
        return carry

    lax.fori_loop(0, panel_count, launch, 0)
    first_time = panel * obs_count * slab

    def two_bins(i, carry):
        table[pl.ds(pl.multiple_of(i * 16, 16), 16), :] = spectra_table(
            bins_ref[2 * i], bins_ref[2 * i + 1], first_time, table.shape[1]
        )
        return carry

    lax.fori_loop(0, NF // 2, two_bins, 0)

    def transform(step):
        own_copy(step).wait()
        for k in range(1, obs_count):
            sample_copy(step, k).wait_recv()
        return jnp.dot(
            table[...], held[step].reshape(table.shape[1], width), preferred_element_type=jnp.float32
        )

    def one_step(step, carry):
        send[step] = transform(step).astype(jnp.bfloat16)
        part_copy(step).start()
        return carry

    lax.fori_loop(0, panel_count - 1, one_step, 0)
    mine[...] = transform(panel_count - 1)

    def add(step, carry):
        part_copy(step).wait_recv()
        mine[...] += arrived[step].astype(jnp.float32)
        return carry

    lax.fori_loop(0, panel_count - 1, add, 0)
    out_ref[obs] = mine[...]
    for k in range(1, obs_count):
        sum_copy(k).start()
    for k in range(1, obs_count):
        sum_copy(k).wait_recv()

    def drain(step, carry):
        for k in range(1, obs_count):
            sample_copy(step, k).wait_send()
        return carry

    lax.fori_loop(0, panel_count, drain, 0)

    def drain_parts(step, carry):
        part_copy(step).wait_send()
        return carry

    lax.fori_loop(0, panel_count - 1, drain_parts, 0)
    for k in range(1, obs_count):
        sum_copy(k).wait_send()


def all_spectra(samples, freq_bins, panel_count, obs_count):
    slab, channels, panels = samples.shape
    width = panels // (panel_count * obs_count)
    rows = 2 * NF * channels
    depth = slab * channels * obs_count
    dma = pltpu.SemaphoreType.DMA
    return pl.pallas_call(
        functools.partial(spectra_kernel, (panel_count, obs_count), width),
        out_shape=jax.ShapeDtypeStruct((obs_count, rows, width), jnp.float32),
        in_specs=[pl.BlockSpec(memory_space=pl.ANY), pl.BlockSpec(memory_space=pltpu.SMEM)],
        out_specs=pl.BlockSpec(memory_space=pltpu.VMEM),
        scratch_shapes=[
            pltpu.VMEM((rows, depth), jnp.bfloat16),
            pltpu.VMEM((panel_count, obs_count, slab, channels, width), jnp.bfloat16),
            pltpu.VMEM((rows, width), jnp.float32),
            pltpu.VMEM((panel_count - 1, rows, width), jnp.bfloat16),
            pltpu.VMEM((panel_count - 1, rows, width), jnp.bfloat16),
            dma((panel_count,)),
            dma((obs_count - 1, panel_count)),
            dma((obs_count - 1, panel_count)),
            dma((panel_count - 1,)),
            dma((panel_count - 1,)),
            dma((obs_count - 1,)),
            dma((obs_count - 1,)),
        ],
        compiler_params=pltpu.CompilerParams(
            collective_id=0, has_side_effects=True, vmem_limit_bytes=40 * 1024 * 1024
        ),
        name="spectra",
    )(samples, freq_bins)


def collect_kernel(panel_count, field_ref, out_ref, staged, arrived, send_sem, recv_sem):
    panel, obs = lax.axis_index("panel"), lax.axis_index("obs")
    rows = staged.shape[1]

    barrier = pltpu.get_barrier_semaphore()

    def greet(k, carry):
        pl.semaphore_signal(barrier, inc=1, device_id=(lax.rem(panel + k, panel_count), obs), device_id_type=MESH)
        return carry

    lax.fori_loop(1, panel_count, greet, 0)
    field = field_ref[...]
    turned = jnp.concatenate([field, jnp.zeros((128 - field.shape[0], field.shape[1]), jnp.float32)], axis=0).T
    for b in range(panel_count):
        staged[b] = turned[b * rows : (b + 1) * rows]

    def copy(k):
        other = lax.rem(panel + k, panel_count)
        return pltpu.make_async_remote_copy(
            src_ref=staged.at[other],
            dst_ref=arrived.at[k - 1],
            send_sem=send_sem.at[k - 1],
            recv_sem=recv_sem.at[k - 1],
            device_id=(other, obs),
            device_id_type=MESH,
        )

    pl.semaphore_wait(barrier, panel_count - 1)

    def launch(k, carry):
        copy(k).start()
        return carry

    lax.fori_loop(1, panel_count, launch, 0)

    def add(k, total):
        copy(k).wait_recv()
        return total + arrived[k - 1]

    total = lax.fori_loop(1, panel_count, add, staged[panel])
    out_ref[...] = total

    def drain(k, carry):
        copy(k).wait_send()
        return carry

    lax.fori_loop(1, panel_count, drain, 0)


def collect(field, panel_count):
    rows = field.shape[1] // panel_count
    dma = pltpu.SemaphoreType.DMA
    vm = pl.BlockSpec(memory_space=pltpu.VMEM)
    return pl.pallas_call(
        functools.partial(collect_kernel, panel_count),
        out_shape=jax.ShapeDtypeStruct((rows, 128), jnp.float32),
        in_specs=[vm],
        out_specs=vm,
        scratch_shapes=[
            pltpu.VMEM((panel_count, rows, 128), jnp.float32),
            pltpu.VMEM((panel_count - 1, rows, 128), jnp.float32),
            dma((panel_count - 1,)),
            dma((panel_count - 1,)),
        ],
        compiler_params=pltpu.CompilerParams(
            collective_id=1, has_side_effects=True, vmem_limit_bytes=16 * 1024 * 1024
        ),
        name="collect",
    )(field)


def shards(samples, panel_position, panel_area, panel_counts, obs_position, freq_bins):
    panel_count = lax.axis_size("panel")
    obs_count = lax.axis_size("obs")
    spectra = all_spectra(samples, freq_bins, panel_count, obs_count)
    field = radiate(
        obs_position, panel_position, panel_area, live_rows(panel_counts), spectra, freq_bins
    )
    total = collect(field, panel_count)[:, : 2 * NF]
    return total.T.reshape(2, NF, -1)


def solution(mesh):
    in_specs = (
        P(("panel", "obs"), None, None),
        P(None, "panel"),
        P("panel"),
        P("panel"),
        P(None, "obs"),
        P(),
    )
    out_specs = P(None, None, ("obs", "panel"))
    return jax.shard_map(shards, mesh=mesh, in_specs=in_specs, out_specs=out_specs, check_vma=False)
```
